128 devices in a mesh: dp: 16 (over x_lo, y, core), tensor: 8 (over x_hi, z).
Axes of the slice: x: 4 (x_hi: 2, x_lo: 2; x = x_hi * 2 + x_lo), y: 4, z: 4, core: 2. Of those that a mesh axis runs over, the one named last changes fastest.
Arguments:
- activations: bfloat16 [4096, 14336], P('dp', 'tensor'), may hold values from -6 to 6
- quant_act: bfloat16 [4096, 14336], P('dp', 'tensor'), may hold values from -6 to 6
- act_scale: float32 [4096, 112], P('dp', 'tensor'), may hold values from 0.1 to 1
- act_mask: int32 [4096, 14336], P('dp', 'tensor'), may hold values 0 or 1
- quant_weight: bfloat16 [4096, 14336], P('dp', 'tensor'), may hold values from -0.046875 to 0.046875
- weight_mask: int32 [4096, 14336], P('dp', 'tensor'), may hold values 0 or 1
- grad_out: bfloat16 [4096, 4096], P('dp'), may hold values from -6 to 6
Outputs:
- grad_act: bfloat16 [4096, 14336], P('dp', 'tensor')
- grad_scale: float32 [4096, 112], P('dp', 'tensor')
- grad_weight: bfloat16 [4096, 14336], P('dp', 'tensor')
The draws below stay inside these ranges and needn't reach their ends.
All inputs are finite; a program needn't handle non-finite values. No bound on the sum of `act_mask` or of `weight_mask` on one device may be relied on, other than what follows from the above.
Results may differ from the reference program's by a relative error of at most 0.023.
Values may be sent and summed in bfloat16 or wider, within the bound.
A program may use at most 128 MiB of HBM per device.

```python
import math
import jax
import jax.numpy as jnp
from jax import lax

D = 4096
FF = 14336
GROUP = 128
TOK_DEV = 256
TOKENS = 4096
GROUPS = 112
N_DP = 16
N_TENSOR = 8


def place_ends(values, stream_key, smallest, high):
    longest = values.shape.index(max(values.shape))
    spots = []
    for shift in (0, 1):
        where = [jax.random.randint(jax.random.fold_in(stream_key, axis), (), 0, length) for axis, length in enumerate(values.shape)]
        where[longest] = (where[longest] + shift) % values.shape[longest]
        spots.append(tuple(where))
    return values.at[spots[0]].set(smallest).at[spots[1]].set(high)


def strengthened(values, key, source, target, shards_of, factor):
    def block_of(axis_at):
        return (jnp.arange(values.shape[axis_at]) // (values.shape[axis_at] // shards_of)).reshape((-1,) + (1,) * (values.ndim - 1 - axis_at))

    near = jax.random.permutation(key, shards_of)[block_of(target)]
    other_side = (block_of(target) + shards_of // 2) % shards_of
    return jnp.where((block_of(source) == near) | (block_of(source) == other_side), factor * values, values)


def level_of(stream_key, shape, split, low, high):
    def one(axis_at, blocks):
        heights = jax.random.uniform(jax.random.fold_in(jax.random.fold_in(stream_key, 6), axis_at), (blocks,), jnp.float32, low / len(split), high / len(split))
        return jnp.repeat(jnp.exp(heights), shape[axis_at] // blocks).reshape((-1,) + (1,) * (len(shape) - axis_at - 1))

    level = one(*split[0])
    for cut in split[1:]:
        level = level * one(*cut)
    return level


def scatter_about(own_key, dims, width, most, split=(), kind=jnp.bfloat16):
    entries = jax.random.normal(own_key, dims, jnp.float32) * width
    if len(split) > 0:
        entries = level_of(own_key, dims, split, -0.22, 0.18) * entries
    return jnp.clip(entries, min=-most, max=most).astype(kind)


def heavy_noise(stream_key, extent, scale, most, pieces, heavy, held_as=jnp.bfloat16):
    entries = scale * jax.random.normal(stream_key, extent, jnp.float32)
    if pieces:
        entries = entries * level_of(stream_key, extent, pieces, -0.22, 0.18)
    return jnp.clip(strengthened(entries, jax.random.fold_in(stream_key, 3), *heavy), -most, most).astype(held_as)


def setup_inputs(seed: int = 0) -> dict:
    seeds = jax.random.split(jax.random.key(seed), 8)
    activations = scatter_about(seeds[0], (TOKENS, FF), 1.0, 6.0, ((0, 16), (1, 8)))
    quant_act = scatter_about(seeds[1], (TOKENS, FF), 1.0, 6.0, ((0, 16), (1, 8)))
    act_scale = jnp.clip(jnp.exp(math.log(1.0) - 2.3025851 * jax.random.uniform(seeds[2], (TOKENS, GROUPS), jnp.float32) ** level_of(seeds[2], (TOKENS, GROUPS), ((0, 16), (1, 8)), -0.2, 0.2)), 0.1, 1.0)
    act_mask = place_ends((jax.random.randint(seeds[3], (TOKENS, FF), 0, 5) < 4).astype(jnp.int32), jax.random.fold_in(seeds[3], 1), 0, 1)
    quant_weight = scatter_about(seeds[4], (D, FF), FF ** -0.5, 0.046875, ((0, 16), (1, 8)))
    weight_mask = place_ends((jax.random.randint(seeds[5], (D, FF), 0, 10) < 9).astype(jnp.int32), jax.random.fold_in(seeds[5], 1), 0, 1)
    grad_out = heavy_noise(seeds[6], (TOKENS, D), 1.0, 6.0, ((0, 16),), (0, 1, 16, 2.0))
    return {"activations": activations, "quant_act": quant_act, "act_scale": act_scale, "act_mask": act_mask, "quant_weight": quant_weight, "weight_mask": weight_mask, "grad_out": grad_out}


def sign_table(count):
    index = jnp.arange(count)
    table = jnp.ones((count, count), jnp.float32)
    for level in range(count.bit_length() - 1):
        bit_row = index // 2 ** level % 2
        table = table * (1.0 - 2.0 * (bit_row[:, None] * bit_row[None, :]).astype(jnp.float32))
    return table / math.sqrt(count)

def rotate(values):
    rows = values.shape[0]
    blocks = values.reshape(rows, N_TENSOR, FF // (N_TENSOR * GROUP), GROUP)
    mixed = jnp.einsum('tnbj,jk->tnbk', blocks, sign_table(GROUP), precision=lax.Precision.HIGHEST)
    mixed = jnp.einsum('tnbk,nm->tmbk', mixed, sign_table(N_TENSOR), precision=lax.Precision.HIGHEST)
    return mixed.reshape(rows, FF)

def reference(activations, quant_act, act_scale, act_mask, quant_weight, weight_mask, grad_out):
    rotated = rotate(activations.astype(jnp.float32))
    grad_quant = jnp.dot(grad_out, quant_weight, preferred_element_type=jnp.float32)
    mask_float = act_mask.astype(jnp.float32)
    grad_rot = mask_float * grad_quant
    grad_act = rotate(grad_rot).astype(jnp.bfloat16)
    spread = grad_quant * (quant_act.astype(jnp.float32) - mask_float * rotated)
    grouped = lax.optimization_barrier(jnp.sum(spread.reshape(TOKENS, GROUPS, GROUP), axis=2))
    grad_scale = grouped / (act_scale * math.sqrt(7.0 * GROUP))
    out_blocks = grad_out.reshape(N_DP, TOK_DEV, D)
    act_blocks = quant_act.reshape(N_DP, TOK_DEV, FF)

    def accumulate(total, pair):
        partial_value = lax.dot_general(pair[0], pair[1], (((0,), (0,)), ((), ())), preferred_element_type=jnp.float32)
        return (total + partial_value.astype(jnp.bfloat16).astype(jnp.float32), None)
    summed, _ = lax.scan(accumulate, jnp.zeros((D, FF), jnp.float32), (out_blocks, act_blocks))
    grad_weight = (weight_mask.astype(jnp.float32) * summed).astype(jnp.bfloat16)
    return (grad_act, grad_scale, grad_weight)
```

```python
import functools

import jax
import jax.numpy as jnp
from jax import lax
from jax.experimental import pallas as pl
from jax.experimental.pallas import tpu as pltpu
from jax.sharding import PartitionSpec as P

TB = 256
NH = 896
KB = 256
GROUP = 128
QT = 64
GH = NH // GROUP
MESH = pl.DeviceIdType.MESH
F32 = jnp.float32
BF16 = jnp.bfloat16
KPOS = {0: 0, 1: 1, 3: 2, 2: 3}


def kslot(xo, ry):
    return (xo * 4 + KPOS[ry]) * KB


def rslot(xo, co):
    return (xo * 2 + co) * TB


def group_sums(values, table):
    high = values.astype(BF16)
    low = (values - high.astype(F32)).astype(BF16)
    return jnp.dot(high, table, preferred_element_type=F32) + jnp.dot(low, table, preferred_element_type=F32)


def hadamard4(v0, v1, v2, v3):
    a, b, c, d = v0 + v1, v0 - v1, v2 + v3, v2 - v3
    return a + c, b + d, a - c, b - d


def kernel(
    act, qa, scale, mask, w, wmask, go,
    out_act, out_scale, out_weight,
    go_buf, w_buf, qa_buf, qa_oth, mask_v, wmask_v, a_recv, a_mix, gq_acc, gq_send, gq_recv, gqx_send, gqx_recv,
    g_v, g_recv, o_send, t1, s_send, s_recv, rs_send, rs_recv, dw_own, dwx_send, dwx_recv, dw_out, signs, table,
    send_sems, recv_sems, local_sems,
):
    d = lax.axis_index("dp")
    n = lax.axis_index("tensor")
    X, Y, C = d // 8, (d // 2) % 4, d % 2
    h, z = n // 4, n % 4

    def at(x, y, c):
        return ((x * 4 + y) * 2 + c, n)

    def member(delta):
        return (n + delta) % 8

    sibling = at(X, Y, 1 - C)
    x_side = at(1 - X, Y, C)
    y_up, y_down = at(X, (Y + 1) % 4, C), at(X, (Y + 3) % 4, C)
    z_up, z_down = (d, h * 4 + (z + 1) % 4), (d, h * 4 + (z + 3) % 4)
    own = pl.ds(pl.multiple_of(X * NH, 128), NH)
    oth = pl.ds(pl.multiple_of((1 - X) * NH, 128), NH)
    cols = (own, oth)

    started = []
    count = [0, 0]

    def remote(src, dst, device):
        i = count[0]
        count[0] += 1
        copy = pltpu.make_async_remote_copy(
            src_ref=src, dst_ref=dst, send_sem=send_sems.at[i], recv_sem=recv_sems.at[i], device_id=device, device_id_type=MESH
        )
        copy.start()
        started.append(copy)
        return copy

    def local(src, dst):
        i = count[1]
        count[1] += 1
        copy = pltpu.make_async_copy(src, dst, local_sems.at[i])
        copy.start()
        return copy

    def slice_rows(zz):
        return pl.ds(pl.multiple_of(zz * QT, QT), QT)

    barrier = pltpu.get_barrier_semaphore()
    partners = [sibling, x_side, y_up, y_down] + [(d, member(delta)) for delta in range(1, 8)]
    for partner in partners:
        pl.semaphore_signal(barrier, inc=1, device_id=partner, device_id_type=MESH)

    def k_columns(xo, ry, c):
        x = X if xo == 0 else 1 - X
        return pl.ds(pl.multiple_of(((x * 4 + (Y + ry) % 4) * 2 + c) * KB, KB), KB)

    blocks = [(xo, ry) for xo in (0, 1) for ry in (0, 1, 3, 2)]
    go_own = [local(go.at[:, k_columns(xo, ry, C)], go_buf.at[pl.ds(rslot(0, 0), TB), pl.ds(kslot(xo, ry), KB)]) for xo, ry in blocks]
    w_own = local(w.at[:, own], w_buf.at[pl.ds(kslot(0, 0), KB)])
    qa_own = local(qa.at[:, own], qa_buf.at[pl.ds(rslot(0, 0), TB)])
    qa_oth_in = local(qa.at[:, oth], qa_oth)
    a_own = [local(act.at[slice_rows(z), cols[hf]], a_recv.at[z, hf]) for hf in (0, 1)]
    mask_in = [local(mask.at[:, cols[hf]], mask_v.at[hf]) for hf in (0, 1)]
    wmask_in = [local(wmask.at[:, cols[hf]], wmask_v.at[hf]) for hf in (0, 1)]
    pl.semaphore_wait(barrier, len(partners))

    w_x = remote(w.at[:, oth], w_buf.at[pl.ds(kslot(1, 0), KB)], x_side)
    w_up = [remote(w.at[:, own], w_buf.at[pl.ds(kslot(0, 3), KB)], y_up), None]
    w_down = [remote(w.at[:, own], w_buf.at[pl.ds(kslot(0, 1), KB)], y_down), None]
    go_sib = [
        remote(go.at[:, k_columns(xo, ry, 1 - C)], go_buf.at[pl.ds(rslot(0, 1), TB), pl.ds(kslot(xo, ry), KB)], sibling)
        for xo, ry in blocks
    ]
    a_in = [
        remote(act.at[slice_rows((z + delta) % 4), cols[hf]], a_recv.at[z, hf], (d, h * 4 + (z + delta) % 4))
        for delta in (1, 2, 3)
        for hf in (0, 1)
    ]
    qa_sib = remote(qa.at[:, own], qa_buf.at[pl.ds(rslot(0, 1), TB)], sibling)

    bits = lax.broadcasted_iota(jnp.int32, (GROUP, GROUP), 0) & lax.broadcasted_iota(jnp.int32, (GROUP, GROUP), 1)
    bits = bits ^ (bits >> 4)
    bits = bits ^ (bits >> 2)
    bits = bits ^ (bits >> 1)
    signs[...] = (1 - 2 * (bits & 1)).astype(F32).astype(BF16)
    for hf in (0, 1):
        first = (X if hf == 0 else 1 - X) * GH
        group = lax.broadcasted_iota(jnp.int32, (NH, GROUP), 0) // GROUP + first
        table[hf] = (group == lax.broadcasted_iota(jnp.int32, (NH, GROUP), 1)).astype(F32).astype(BF16)

    def quarter(xo, co):
        return pl.ds(pl.multiple_of(rslot(xo, co) + z * QT, QT), QT)

    def go_cross(co):
        return [
            remote(
                go_buf.at[quarter(0, co), pl.ds(xo * 4 * KB, 4 * KB)],
                go_buf.at[quarter(1, co), pl.ds((1 - xo) * 4 * KB, 4 * KB)],
                x_side,
            )
            for xo in (0, 1)
        ]

    for copy in go_own:
        copy.wait()
    go_x = [go_cross(0), None]
    for copy in go_sib:
        copy.wait_recv()
    go_x[1] = go_cross(1)

    w_x.wait_recv()
    slot = w_buf.at[pl.ds(kslot(1, 0), KB)]
    w_up[1] = remote(slot, w_buf.at[pl.ds(kslot(1, 3), KB)], y_up)
    w_down[1] = remote(slot, w_buf.at[pl.ds(kslot(1, 1), KB)], y_down)
    w_up[0].wait_recv()
    w_far0 = remote(w_buf.at[pl.ds(kslot(0, 3), KB)], w_buf.at[pl.ds(kslot(0, 2), KB)], y_up)

    go_up, go_down = [], []
    for co in (0, 1):
        for copy in go_x[co]:
            copy.wait_recv()
        here = go_buf.at[quarter(1, co)]
        go_up.append(remote(here, here, z_up))
        go_down.append(remote(here, here, z_down))
    qa_x = remote(qa.at[:, oth], qa_buf.at[pl.ds(rslot(1, 0), TB)], x_side)

    for copy in a_own:
        copy.wait()
    for copy in a_in:
        copy.wait_recv()
    for hf in (0, 1):
        mixed = hadamard4(*[a_recv[zz, hf].astype(F32) for zz in range(4)])
        for zz in range(4):
            a_mix[zz, hf] = mixed[zz]

    w_down[1].wait_recv()
    w_far1 = remote(w_buf.at[pl.ds(kslot(1, 1), KB)], w_buf.at[pl.ds(kslot(1, 2), KB)], y_down)

    def quarter_of(zz, co):
        return pl.ds(pl.multiple_of(rslot(1, co) + (zz % 4) * QT, QT), QT)

    go_up[0].wait_recv()
    passed = go_buf.at[quarter_of(z + 3, 0)]
    go_far0 = remote(passed, passed, z_up)
    go_down[1].wait_recv()
    passed = go_buf.at[quarter_of(z + 1, 1)]
    go_far1 = remote(passed, passed, z_down)

    qa_x.wait_recv()
    qa_far = remote(qa_buf.at[pl.ds(rslot(1, 0), TB)], qa_buf.at[pl.ds(rslot(1, 1), TB)], sibling)

    w_own.wait()
    w_down[0].wait_recv()
    w_up[1].wait_recv()
    w_far0.wait_recv()
    w_far1.wait_recv()
    go_down[0].wait_recv()
    go_up[1].wait_recv()
    go_far0.wait_recv()
    go_far1.wait_recv()
    qa_own.wait()
    qa_sib.wait_recv()
    qa_far.wait_recv()

    def weight_block(xo, ry):
        return lax.dot_general(
            go_buf[:, kslot(xo, ry) : kslot(xo, ry) + KB], qa_buf[...], (((0,), (0,)), ((), ())), preferred_element_type=F32
        )

    rs_send[0] = weight_block(0, 2).astype(BF16)
    rs_far0 = remote(rs_send.at[0], rs_recv.at[0], y_up)
    rs_send[1] = weight_block(1, 2).astype(BF16)
    rs_far1 = remote(rs_send.at[1], rs_recv.at[1], y_down)

    def quant_rows(xo, co):
        return jnp.dot(go_buf[rslot(xo, co) : rslot(xo, co) + TB], w_buf[...], preferred_element_type=F32)

    gq_sib = [None, None]
    for xo in (1, 0):
        gq_send[xo] = quant_rows(xo, 1).astype(BF16)
        gq_sib[xo] = remote(gq_send.at[xo], gq_recv.at[xo], sibling)
    for xo in (1, 0):
        gq_acc[xo] = quant_rows(xo, 0)
    gq_sib[1].wait_recv()
    gqx_send[...] = (gq_acc[1] + gq_recv[1].astype(F32)).astype(BF16)
    gq_x = remote(gqx_send, gqx_recv, x_side)

    for copy in mask_in:
        copy.wait()
    qa_oth_in.wait()

    def rotate_half(hf, quant, quantized):
        wide = quant.astype(F32)
        sums = group_sums(wide * quantized.astype(F32), table[hf])
        if hf == 0:
            t1[...] = sums
        else:
            t1[...] += sums
        rot = (wide * mask_v[hf].astype(F32)).astype(BF16)
        for g in range(GH):
            part = slice(g * GROUP, (g + 1) * GROUP)
            g_v[hf, :, part] = jnp.dot(rot[:, part], signs[...], preferred_element_type=F32).astype(BF16)
        copies = []
        for delta in range(1, 8):
            to = member(delta)
            copies.append(remote(g_v.at[hf, slice_rows(to % 4)], g_recv.at[n, hf], (d, to)))
        return copies, local(g_v.at[hf, slice_rows(z)], g_recv.at[n, hf])

    gq_sib[0].wait_recv()
    g_in = [None, None]
    g_in[0] = rotate_half(0, (gq_acc[0] + gq_recv[0].astype(F32)).astype(BF16), qa_buf[0:TB])

    rs_send[2] = weight_block(1, 1).astype(BF16)
    rs_near_up1 = remote(rs_send.at[2], rs_recv.at[2], y_up)
    rs_send[3] = weight_block(0, 3).astype(BF16)
    rs_near_down0 = remote(rs_send.at[3], rs_recv.at[3], y_down)
    for xo in (0, 1):
        dw_own[xo] = weight_block(xo, 0)
    dw_own[2] = weight_block(0, 1)
    dw_own[3] = weight_block(1, 3)
    rs_far0.wait_recv()
    rs_send[4] = (dw_own[2] + rs_recv[0].astype(F32)).astype(BF16)
    rs_near_up0 = remote(rs_send.at[4], rs_recv.at[4], y_up)
    rs_far1.wait_recv()
    rs_send[5] = (dw_own[3] + rs_recv[1].astype(F32)).astype(BF16)
    rs_near_down1 = remote(rs_send.at[5], rs_recv.at[5], y_down)

    gq_x.wait_recv()
    g_in[1] = rotate_half(1, gqx_recv[...], qa_oth[...])

    sign = (1 - 2 * h).astype(F32)

    def mix_half(hf):
        copies, kept = g_in[hf]
        for copy in copies:
            copy.wait_recv()
        kept.wait()
        sums = []
        for zz in range(4):
            low, high = g_recv[zz, hf].astype(F32), g_recv[4 + zz, hf].astype(F32)
            sums.append(low + sign * high)
            for hh, value in ((0, low), (1, sign * high)):
                part = group_sums(value * a_mix[zz, hf], table[hf])
                if hf == 0:
                    s_send[hh * 4 + zz] = part
                else:
                    s_send[hh * 4 + zz] += part
        mixed = hadamard4(*sums)
        for zz in range(4):
            o_send[zz, hf] = (mixed[zz] * (1.0 / 32.0)).astype(BF16)
        copies = []
        for delta in (1, 2, 3):
            to = (z + delta) % 4
            copies.append(remote(o_send.at[to, hf], out_act.at[slice_rows(z), cols[hf]], (d, h * 4 + to)))
        return copies, local(o_send.at[z, hf], out_act.at[slice_rows(z), cols[hf]])

    o_in = [mix_half(0), None]

    rs_near_up1.wait_recv()
    rs_near_down1.wait_recv()
    dwx_send[...] = (dw_own[1] + rs_recv[2].astype(F32) + rs_recv[5].astype(F32)).astype(BF16)
    dw_x = remote(dwx_send, dwx_recv, x_side)
    rs_near_up0.wait_recv()
    rs_near_down0.wait_recv()
    for copy in wmask_in:
        copy.wait()
    dw_out[0] = ((dw_own[0] + rs_recv[3].astype(F32) + rs_recv[4].astype(F32)) * wmask_v[0].astype(F32)).astype(BF16)
    dw_done = [local(dw_out.at[0], out_weight.at[:, own]), None]

    o_in[1] = mix_half(1)
    s_in = [remote(s_send.at[member(delta)], s_recv.at[n], (d, member(delta))) for delta in range(1, 8)]
    s_kept = local(s_send.at[n], s_recv.at[n])

    dw_x.wait_recv()
    dw_out[1] = (dwx_recv[...].astype(F32) * wmask_v[1].astype(F32)).astype(BF16)
    dw_done[1] = local(dw_out.at[1], out_weight.at[:, oth])

    for copy in s_in:
        copy.wait_recv()
    s_kept.wait()
    for zz in range(4):
        rows = slice(zz * QT, (zz + 1) * QT)
        total = t1[rows] - (s_recv[zz] + s_recv[4 + zz]) * (1.0 / 32.0)
        out_scale[rows] = total[:, : 2 * GH] / (scale[rows] * (7.0 * GROUP) ** 0.5)

    for copies, kept in o_in:
        for copy in copies:
            copy.wait_recv()
        kept.wait()
    for copy in dw_done:
        copy.wait()
    for copy in started:
        copy.wait_send()


def shards(activations, quant_act, act_scale, act_mask, quant_weight, weight_mask, grad_out):
    anywhere = pl.BlockSpec(memory_space=pl.ANY)
    vmem = pl.BlockSpec(memory_space=pltpu.VMEM)
    half = (TB, NH)
    return pl.pallas_call(
        kernel,
        out_shape=(
            jax.ShapeDtypeStruct((TB, 2 * NH), BF16),
            jax.ShapeDtypeStruct((TB, 2 * GH), F32),
            jax.ShapeDtypeStruct((TB, 2 * NH), BF16),
        ),
        in_specs=[anywhere, anywhere, vmem, anywhere, anywhere, anywhere, anywhere],
        out_specs=(anywhere, vmem, anywhere),
        scratch_shapes=[
            pltpu.VMEM((4 * TB, 8 * KB), BF16),
            pltpu.VMEM((8 * KB, NH), BF16),
            pltpu.VMEM((4 * TB, NH), BF16),
            pltpu.VMEM(half, BF16),
            pltpu.VMEM((2,) + half, jnp.int32),
            pltpu.VMEM((2,) + half, jnp.int32),
            pltpu.VMEM((4, 2, QT, NH), BF16),
            pltpu.VMEM((4, 2, QT, NH), F32),
            pltpu.VMEM((2,) + half, F32),
            pltpu.VMEM((2,) + half, BF16),
            pltpu.VMEM((2,) + half, BF16),
            pltpu.VMEM(half, BF16),
            pltpu.VMEM(half, BF16),
            pltpu.VMEM((2,) + half, BF16),
            pltpu.VMEM((8, 2, QT, NH), BF16),
            pltpu.VMEM((4, 2, QT, NH), BF16),
            pltpu.VMEM((TB, GROUP), F32),
            pltpu.VMEM((8, QT, GROUP), F32),
            pltpu.VMEM((8, QT, GROUP), F32),
            pltpu.VMEM((6,) + half, BF16),
            pltpu.VMEM((6,) + half, BF16),
            pltpu.VMEM((4,) + half, F32),
            pltpu.VMEM(half, BF16),
            pltpu.VMEM(half, BF16),
            pltpu.VMEM((2,) + half, BF16),
            pltpu.VMEM((GROUP, GROUP), BF16),
            pltpu.VMEM((2, NH, GROUP), BF16),
            pltpu.SemaphoreType.DMA((72,)),
            pltpu.SemaphoreType.DMA((72,)),
            pltpu.SemaphoreType.DMA((32,)),
        ],
        compiler_params=pltpu.CompilerParams(collective_id=0, has_side_effects=True, vmem_limit_bytes=56 * 2**20),
        cost_estimate=pl.CostEstimate(flops=7516192768, bytes_accessed=16 * 2**20, transcendentals=0),
    )(activations, quant_act, act_scale, act_mask, quant_weight, weight_mask, grad_out)


def solution(mesh):
    return jax.shard_map(
        shards,
        mesh=mesh,
        in_specs=(
            P("dp", "tensor"),
            P("dp", "tensor"),
            P("dp", "tensor"),
            P("dp", "tensor"),
            P("dp", "tensor"),
            P("dp", "tensor"),
            P("dp", None),
        ),
        out_specs=(P("dp", "tensor"), P("dp", "tensor"), P("dp", "tensor")),
        check_vma=False,
    )
```

```python
import functools

import jax
import jax.numpy as jnp
from jax import lax
from jax.experimental import pallas as pl
from jax.experimental.pallas import tpu as pltpu
from jax.sharding import PartitionSpec as P

TB = 256
NH = 896
KB = 256
HB = 128
GROUP = 128
QT = 64
GH = NH // GROUP
CHUNKS = ((0, 256), (256, 256), (512, 384))
MESH = pl.DeviceIdType.MESH
F32 = jnp.float32
BF16 = jnp.bfloat16
KPOS = {0: 0, 1: 1, 3: 2, 2: 3}


def kslot(xo, ry):
    return (xo * 4 + KPOS[ry]) * KB


def rslot(xo, co):
    return (xo * 2 + co) * TB


def group_sums(values, table):
    high = values.astype(BF16)
    low = (values - high.astype(F32)).astype(BF16)
    return jnp.dot(high, table, preferred_element_type=F32) + jnp.dot(low, table, preferred_element_type=F32)


def hadamard4(v0, v1, v2, v3):
    a, b, c, d = v0 + v1, v0 - v1, v2 + v3, v2 - v3
    return a + c, b + d, a - c, b - d


def kernel(
    act, qa, scale, mask, w, wmask, go,
    out_act, out_scale, out_weight,
    go_buf, w_buf, qa_buf, qa_oth, mask_v, wmask_v, a_recv, a_mix, gq_part, gq_send, gq_recv, gqx_send, gqx_recv,
    g_v, g_recv, o_send, t1, p_v, s_send, s_recv, rs_send, rs_recv, dw_own, dw_near, dwx_send, dwx_recv, dw_out, signs, table,
    send_sems, recv_sems, local_sems,
):
    d = lax.axis_index("dp")
    n = lax.axis_index("tensor")
    X, Y, C = d // 8, (d // 2) % 4, d % 2
    h, z = n // 4, n % 4

    def at(x, y, c):
        return ((x * 4 + y) * 2 + c, n)

    def member(delta):
        return (n + delta) % 8

    sibling = at(X, Y, 1 - C)
    x_side = at(1 - X, Y, C)
    x_across = (((1 - X) * 4 + Y) * 2 + C, (n + 4) % 8)
    y_up, y_down = at(X, (Y + 1) % 4, C), at(X, (Y + 3) % 4, C)
    z_up, z_down = (d, h * 4 + (z + 1) % 4), (d, h * 4 + (z + 3) % 4)
    own = pl.ds(pl.multiple_of(X * NH, 128), NH)
    oth = pl.ds(pl.multiple_of((1 - X) * NH, 128), NH)
    cols = (own, oth)

    def columns(hf, c):
        base = (X if hf == 0 else 1 - X) * NH
        return pl.ds(pl.multiple_of(base + CHUNKS[c][0], 128), CHUNKS[c][1])

    started = []
    count = [0, 0]

    def remote(src, dst, device):
        i = count[0]
        count[0] += 1
        copy = pltpu.make_async_remote_copy(
            src_ref=src, dst_ref=dst, send_sem=send_sems.at[i], recv_sem=recv_sems.at[i], device_id=device, device_id_type=MESH
        )
        copy.start()
        started.append(copy)
        return copy

    def local(src, dst):
        i = count[1]
        count[1] += 1
        copy = pltpu.make_async_copy(src, dst, local_sems.at[i])
        copy.start()
        return copy

    def slice_rows(zz):
        return pl.ds(pl.multiple_of(zz * QT, QT), QT)

    barrier = pltpu.get_barrier_semaphore()
    partners = [sibling, x_side, x_across, y_up, y_down] + [(d, member(delta)) for delta in range(1, 8)]
    for partner in partners:
        pl.semaphore_signal(barrier, inc=1, device_id=partner, device_id_type=MESH)

    def k_columns(xo, ry, c):
        x = X if xo == 0 else 1 - X
        return pl.ds(pl.multiple_of(((x * 4 + (Y + ry) % 4) * 2 + c) * KB, KB), KB)

    blocks = [(xo, ry) for xo in (0, 1) for ry in (0, 1, 3, 2)]
    go_own = [local(go.at[:, k_columns(xo, ry, C)], go_buf.at[pl.ds(rslot(0, 0), TB), pl.ds(kslot(xo, ry), KB)]) for xo, ry in blocks]
    w_own = local(w.at[:, own], w_buf.at[pl.ds(kslot(0, 0), KB)])
    qa_own = local(qa.at[:, own], qa_buf.at[pl.ds(rslot(0, 0), TB)])
    qa_oth_in = local(qa.at[:, oth], qa_oth)
    a_own = [local(act.at[slice_rows(z), cols[hf]], a_recv.at[z, hf]) for hf in (0, 1)]
    mask_in = [local(mask.at[:, cols[hf]], mask_v.at[hf]) for hf in (0, 1)]
    wmask_in = [local(wmask.at[:, cols[hf]], wmask_v.at[hf]) for hf in (0, 1)]
    pl.semaphore_wait(barrier, len(partners))

    def inner(c):
        return pl.ds(*CHUNKS[c])

    def w_cross(c):
        return remote(w.at[:, columns(1, c)], w_buf.at[pl.ds(kslot(1, 0), KB), inner(c)], x_side)

    def w_first(c, ry, device):
        return remote(w.at[:, columns(0, c)], w_buf.at[pl.ds(kslot(0, ry), KB), inner(c)], device)

    def w_pass(c, xo, come, go_to, device):
        here = w_buf.at[pl.ds(kslot(xo, come), KB), inner(c)]
        return remote(here, w_buf.at[pl.ds(kslot(xo, go_to), KB), inner(c)], device)

    w_x, w_up0, w_down0, w_up1, w_down1, w_far0, w_far1 = ([None] * 3 for _ in range(7))
    def w_own_pair(c):
        w_up0[c] = w_first(c, 3, y_up)
        w_down0[c] = w_first(c, 1, y_down)

    def w_pass_pair(c):
        w_x[c].wait_recv()
        w_up1[c] = w_pass(c, 1, 0, 3, y_up)
        w_down1[c] = w_pass(c, 1, 0, 1, y_down)

    def w_up_on(c):
        w_up0[c].wait_recv()
        w_far0[c] = w_pass(c, 0, 3, 2, y_up)

    def w_down_on(c):
        w_down1[c].wait_recv()
        w_far1[c] = w_pass(c, 1, 1, 2, y_down)

    def w_complete(c):
        for copy in (w_down0[c], w_up1[c], w_far0[c], w_far1[c]):
            copy.wait_recv()

    w_x[0] = w_cross(0)
    w_own_pair(0)
    go_sib = [
        remote(go.at[:, k_columns(xo, ry, 1 - C)], go_buf.at[pl.ds(rslot(0, 1), TB), pl.ds(kslot(xo, ry), KB)], sibling)
        for xo, ry in blocks
    ]
    a_in = [
        remote(act.at[slice_rows((z + delta) % 4), cols[hf]], a_recv.at[z, hf], (d, h * 4 + (z + delta) % 4))
        for delta in (1, 2, 3)
        for hf in (0, 1)
    ]
    qa_sib = remote(qa.at[:, own], qa_buf.at[pl.ds(rslot(0, 1), TB)], sibling)

    bits = lax.broadcasted_iota(jnp.int32, (GROUP, GROUP), 0) & lax.broadcasted_iota(jnp.int32, (GROUP, GROUP), 1)
    bits = bits ^ (bits >> 4)
    bits = bits ^ (bits >> 2)
    bits = bits ^ (bits >> 1)
    signs[...] = (1 - 2 * (bits & 1)).astype(F32).astype(BF16)
    for hf in (0, 1):
        first = (X if hf == 0 else 1 - X) * GH
        group = lax.broadcasted_iota(jnp.int32, (NH, GROUP), 0) // GROUP + first
        table[hf] = (group == lax.broadcasted_iota(jnp.int32, (NH, GROUP), 1)).astype(F32).astype(BF16)

    def quarter(xo, co, zz):
        return pl.ds(pl.multiple_of(rslot(xo, co) + (zz % 4) * QT, QT), QT)

    def go_cross(co):
        return [
            remote(
                go_buf.at[quarter(0, co, z), pl.ds(xo * 4 * KB, 4 * KB)],
                go_buf.at[quarter(1, co, z), pl.ds((1 - xo) * 4 * KB, 4 * KB)],
                x_across,
            )
            for xo in (0, 1)
        ]

    def go_along(co):
        for copy in go_x[co]:
            copy.wait_recv()
        here = go_buf.at[quarter(1, co, z)]
        return remote(here, here, z_up), remote(here, here, z_down)

    for copy in go_own:
        copy.wait()
    go_x = [go_cross(0), None]
    w_x[1] = w_cross(1)
    w_own_pair(1)
    for copy in go_sib:
        copy.wait_recv()
    go_x[1] = go_cross(1)
    w_pass_pair(0)
    w_x[2] = w_cross(2)
    w_up_on(0)
    go_up, go_down = [None, None], [None, None]
    go_up[0], go_down[0] = go_along(0)
    w_pass_pair(1)
    qa_x = remote(qa.at[:, oth], qa_buf.at[pl.ds(rslot(1, 0), TB)], x_side)
    w_down_on(0)
    w_up_on(1)
    w_own_pair(2)
    go_up[1], go_down[1] = go_along(1)

    for copy in a_own:
        copy.wait()
    for copy in a_in:
        copy.wait_recv()
    for hf in (0, 1):
        mixed = hadamard4(*[a_recv[zz, hf].astype(F32) for zz in range(4)])
        for zz in range(4):
            a_mix[zz, hf] = mixed[zz]

    w_pass_pair(2)

    def quant_rows(xo, co, c):
        first, width = CHUNKS[c]
        return jnp.dot(
            go_buf[rslot(xo, co) : rslot(xo, co) + TB], w_buf[:, first : first + width], preferred_element_type=F32
        )

    gq_sib = {}

    def quant_start(xo, c):
        part = slice(CHUNKS[c][0], sum(CHUNKS[c]))
        gq_send[xo, :, part] = quant_rows(xo, 1, c).astype(BF16)
        gq_sib[xo, c] = remote(gq_send.at[xo, :, inner(c)], gq_recv.at[xo, :, inner(c)], sibling)
        gq_part[xo, :, part] = quant_rows(xo, 0, c)

    def quant_end(xo, c):
        part = slice(CHUNKS[c][0], sum(CHUNKS[c]))
        gq_sib[xo, c].wait_recv()
        return (gq_part[xo, :, part] + gq_recv[xo, :, part].astype(F32)).astype(BF16)

    gq_x = [None] * 3

    def quant_cross(c):
        part = slice(CHUNKS[c][0], sum(CHUNKS[c]))
        gqx_send[:, part] = quant_end(1, c)
        gq_x[c] = remote(gqx_send.at[:, inner(c)], gqx_recv.at[:, inner(c)], x_side)

    g_in = {}

    def rotate(hf, c, quant):
        first, width = CHUNKS[c]
        part = slice(first, first + width)
        wide = quant.astype(F32)
        rot = (wide * mask_v[hf, :, part].astype(F32)).astype(BF16)
        for g in range(width // GROUP):
            g_v[hf, :, first + g * GROUP : first + (g + 1) * GROUP] = jnp.dot(
                rot[:, g * GROUP : (g + 1) * GROUP], signs[...], preferred_element_type=F32
            ).astype(BF16)
        copies = []
        for delta in range(1, 8):
            to = member(delta)
            copies.append(remote(g_v.at[hf, slice_rows(to % 4), inner(c)], g_recv.at[n, hf, :, inner(c)], (d, to)))
        g_in[hf, c] = copies, local(g_v.at[hf, slice_rows(z), inner(c)], g_recv.at[n, hf, :, inner(c)])
        quantized = qa_buf[0:TB, part] if hf == 0 else qa_oth[:, part]
        sums = group_sums(wide * quantized.astype(F32), table[hf, part])
        if hf == 0 and c == 0:
            t1[...] = sums
        else:
            t1[...] += sums

    def weight_block(xo, ry):
        return lax.dot_general(
            go_buf[:, kslot(xo, ry) : kslot(xo, ry) + KB], qa_buf[...], (((0,), (0,)), ((), ())), preferred_element_type=F32
        )

    rs_far, rs_alone, rs_added = {}, {}, {}

    def reduce_far(xo):
        rs_send[xo, 0] = weight_block(xo, 2).astype(BF16)
        rs_far[xo] = [
            remote(rs_send.at[xo, 0, pl.ds(i * HB, HB)], rs_recv.at[xo, 0, pl.ds(i * HB, HB)], (y_up, y_down)[i]) for i in (0, 1)
        ]

    def reduce_near(xo):
        rs_alone[xo] = []
        for i, ry in ((0, 1), (1, 3)):
            value = weight_block(xo, ry)
            dw_near[xo, i] = value[i * HB : (i + 1) * HB]
            rs_send[xo, 1 + i, (1 - i) * HB : (2 - i) * HB] = value[(1 - i) * HB : (2 - i) * HB].astype(BF16)
            part = pl.ds((1 - i) * HB, HB)
            rs_alone[xo].append(remote(rs_send.at[xo, 1 + i, part], rs_recv.at[xo, 1 + i, part], (y_up, y_down)[i]))

    def reduce_pass(xo):
        rs_added[xo] = []
        for i in (0, 1):
            rs_far[xo][i].wait_recv()
            rows = slice(i * HB, (i + 1) * HB)
            rs_send[xo, 1 + i, rows] = (dw_near[xo, i] + rs_recv[xo, 0, rows].astype(F32)).astype(BF16)
            part = pl.ds(i * HB, HB)
            rs_added[xo].append(remote(rs_send.at[xo, 1 + i, part], rs_recv.at[xo, 1 + i, part], (y_up, y_down)[i]))

    def reduce_end(xo):
        for copy in rs_alone[xo] + rs_added[xo]:
            copy.wait_recv()
        return dw_own[xo] + rs_recv[xo, 1].astype(F32) + rs_recv[xo, 2].astype(F32)

    w_own.wait()
    w_complete(0)
    quant_start(0, 0)
    w_down_on(1)
    go_up[0].wait_recv()
    passed = go_buf.at[quarter(1, 0, z + 3)]
    go_far0 = remote(passed, passed, z_up)
    for copy in mask_in:
        copy.wait()
    qa_own.wait()
    qa_oth_in.wait()
    rotate(0, 0, quant_end(0, 0))
    w_up_on(2)
    go_down[1].wait_recv()
    passed = go_buf.at[quarter(1, 1, z + 1)]
    go_far1 = remote(passed, passed, z_down)
    qa_x.wait_recv()
    qa_far = remote(qa_buf.at[pl.ds(rslot(1, 0), TB)], qa_buf.at[pl.ds(rslot(1, 1), TB)], sibling)
    w_complete(1)
    quant_start(0, 1)
    w_down_on(2)
    rotate(0, 1, quant_end(0, 1))
    for copy in (go_down[0], go_up[1], go_far0, go_far1):
        copy.wait_recv()
    quant_start(1, 0)
    qa_sib.wait_recv()
    qa_far.wait_recv()
    reduce_far(1)
    quant_cross(0)
    quant_start(1, 1)
    reduce_near(1)
    quant_cross(1)
    w_complete(2)
    quant_start(0, 2)
    reduce_far(0)
    rotate(0, 2, quant_end(0, 2))
    quant_start(1, 2)
    reduce_near(0)
    quant_cross(2)
    gq_x[0].wait_recv()
    rotate(1, 0, gqx_recv[:, 0:256])
    reduce_pass(1)
    gq_x[1].wait_recv()
    rotate(1, 1, gqx_recv[:, 256:512])
    reduce_pass(0)
    dw_own[1] = weight_block(1, 0)
    dw_own[0] = weight_block(0, 0)

    sign = (1 - 2 * h).astype(F32)

    o_in = []

    def mix(hf, c):
        first, width = CHUNKS[c]
        part = slice(first, first + width)
        copies, kept = g_in[hf, c]
        for copy in copies:
            copy.wait_recv()
        kept.wait()
        sums = []
        for zz in range(4):
            sums.append(g_recv[zz, hf, :, part].astype(F32) + sign * g_recv[4 + zz, hf, :, part].astype(F32))
        mixed = hadamard4(*sums)
        for zz in range(4):
            o_send[zz, hf, :, part] = (mixed[zz] * (1.0 / 32.0)).astype(BF16)
        copies = []
        for delta in (1, 2, 3):
            to = (z + delta) % 4
            copies.append(remote(o_send.at[to, hf, :, inner(c)], out_act.at[slice_rows(z), columns(hf, c)], (d, h * 4 + to)))
        o_in.append((copies, local(o_send.at[z, hf, :, inner(c)], out_act.at[slice_rows(z), columns(hf, c)])))
        for m in range(8):
            value = g_recv[m, hf, :, part].astype(F32) * a_mix[m % 4, hf, :, part]
            top = value.astype(BF16)
            rows = slice(m * QT, (m + 1) * QT)
            p_v[0, rows, part] = top
            p_v[1, rows, part] = (value - top.astype(F32)).astype(BF16)
        sums = jnp.dot(p_v[0, :, part], table[hf, part], preferred_element_type=F32)
        sums += jnp.dot(p_v[1, :, part], table[hf, part], preferred_element_type=F32)
        if hf == 0 and c == 0:
            s_send[...] = sums
        else:
            s_send[...] += sums

    mix(0, 0)
    gq_x[2].wait_recv()
    rotate(1, 2, gqx_recv[:, 512:896])
    mix(0, 1)
    mix(0, 2)
    dwx_send[...] = reduce_end(1).astype(BF16)
    dw_x = remote(dwx_send, dwx_recv, x_side)
    mix(1, 0)
    mix(1, 1)
    mix(1, 2)
    s_send[4 * QT :] *= sign
    s_in = [
        remote(s_send.at[pl.ds(pl.multiple_of(member(delta) * QT, QT), QT)], s_recv.at[n], (d, member(delta))) for delta in range(1, 8)
    ]
    s_kept = local(s_send.at[pl.ds(pl.multiple_of(n * QT, QT), QT)], s_recv.at[n])

    for copy in wmask_in:
        copy.wait()
    dw_out[0] = (reduce_end(0) * wmask_v[0].astype(F32)).astype(BF16)
    dw_done = [local(dw_out.at[0], out_weight.at[:, own]), None]

    dw_x.wait_recv()
    dw_out[1] = (dwx_recv[...].astype(F32) * wmask_v[1].astype(F32)).astype(BF16)
    dw_done[1] = local(dw_out.at[1], out_weight.at[:, oth])

    for copy in s_in:
        copy.wait_recv()
    s_kept.wait()
    for zz in range(4):
        rows = slice(zz * QT, (zz + 1) * QT)
        t1[rows] -= (s_recv[zz] + s_recv[4 + zz]) * (1.0 / 32.0)
    out_scale[...] = t1[...].T[: 2 * GH] / (scale[...] * (7.0 * GROUP) ** 0.5)

    for copies, kept in o_in:
        for copy in copies:
            copy.wait_recv()
        kept.wait()
    for copy in dw_done:
        copy.wait()
    for copy in started:
        copy.wait_send()


def shards(activations, quant_act, act_scale, act_mask, quant_weight, weight_mask, grad_out):
    anywhere = pl.BlockSpec(memory_space=pl.ANY)
    vmem = pl.BlockSpec(memory_space=pltpu.VMEM)
    half = (TB, NH)
    grad_act, grad_scale, grad_weight = pl.pallas_call(
        kernel,
        out_shape=(
            jax.ShapeDtypeStruct((TB, 2 * NH), BF16),
            jax.ShapeDtypeStruct((2 * GH, TB), F32),
            jax.ShapeDtypeStruct((TB, 2 * NH), BF16),
        ),
        in_specs=[anywhere, anywhere, vmem, anywhere, anywhere, anywhere, anywhere],
        out_specs=(anywhere, vmem, anywhere),
        scratch_shapes=[
            pltpu.VMEM((4 * TB, 8 * KB), BF16),
            pltpu.VMEM((8 * KB, NH), BF16),
            pltpu.VMEM((4 * TB, NH), BF16),
            pltpu.VMEM(half, BF16),
            pltpu.VMEM((2,) + half, jnp.int32),
            pltpu.VMEM((2,) + half, jnp.int32),
            pltpu.VMEM((4, 2, QT, NH), BF16),
            pltpu.VMEM((4, 2, QT, NH), F32),
            pltpu.VMEM((2,) + half, F32),
            pltpu.VMEM((2,) + half, BF16),
            pltpu.VMEM((2,) + half, BF16),
            pltpu.VMEM(half, BF16),
            pltpu.VMEM(half, BF16),
            pltpu.VMEM((2,) + half, BF16),
            pltpu.VMEM((8, 2, QT, NH), BF16),
            pltpu.VMEM((4, 2, QT, NH), BF16),
            pltpu.VMEM((TB, GROUP), F32),
            pltpu.VMEM((2, 8 * QT, NH), BF16),
            pltpu.VMEM((8 * QT, GROUP), F32),
            pltpu.VMEM((8, QT, GROUP), F32),
            pltpu.VMEM((2, 3) + half, BF16),
            pltpu.VMEM((2, 3) + half, BF16),
            pltpu.VMEM((2,) + half, F32),
            pltpu.VMEM((2, 2, HB, NH), F32),
            pltpu.VMEM(half, BF16),
            pltpu.VMEM(half, BF16),
            pltpu.VMEM((2,) + half, BF16),
            pltpu.VMEM((GROUP, GROUP), BF16),
            pltpu.VMEM((2, NH, GROUP), BF16),
            pltpu.SemaphoreType.DMA((176,)),
            pltpu.SemaphoreType.DMA((176,)),
            pltpu.SemaphoreType.DMA((32,)),
        ],
        compiler_params=pltpu.CompilerParams(collective_id=0, has_side_effects=True, vmem_limit_bytes=56 * 2**20),
        cost_estimate=pl.CostEstimate(flops=7516192768, bytes_accessed=16 * 2**20, transcendentals=0),
    )(activations, quant_act, act_scale.T, act_mask, quant_weight, weight_mask, grad_out)
    return grad_act, grad_scale.T, grad_weight


def solution(mesh):
    return jax.shard_map(
        shards,
        mesh=mesh,
        in_specs=(
            P("dp", "tensor"),
            P("dp", "tensor"),
            P("dp", "tensor"),
            P("dp", "tensor"),
            P("dp", "tensor"),
            P("dp", "tensor"),
            P("dp", None),
        ),
        out_specs=(P("dp", "tensor"), P("dp", "tensor"), P("dp", "tensor")),
        check_vma=False,
    )
```

```python
import functools

import jax
import jax.numpy as jnp
from jax import lax
from jax.experimental import pallas as pl
from jax.experimental.pallas import tpu as pltpu
from jax.sharding import PartitionSpec as P

TB = 256
NH = 896
KB = 256
HB = 128
GROUP = 128
QT = 64
GH = NH // GROUP
CHUNKS = ((0, 256), (256, 256), (512, 384))
PARTS = 4
MESH = pl.DeviceIdType.MESH
F32 = jnp.float32
BF16 = jnp.bfloat16
KPOS = {0: 0, 1: 1, 3: 2, 2: 3}


def kslot(xo, ry):
    return (xo * 4 + KPOS[ry]) * KB


def rslot(xo, co):
    return (xo * 2 + co) * TB


def group_sums(values, table):
    high = values.astype(BF16)
    low = (values - high.astype(F32)).astype(BF16)
    return jnp.dot(high, table, preferred_element_type=F32) + jnp.dot(low, table, preferred_element_type=F32)


def hadamard4(v0, v1, v2, v3):
    a, b, c, d = v0 + v1, v0 - v1, v2 + v3, v2 - v3
    return a + c, b + d, a - c, b - d


def kernel(
    act, qa, scale, mask, w, wmask, go,
    out_act, out_scale, out_weight,
    go_buf, w_buf, qa_buf, qa_oth, mask_v, wmask_v, a_recv, a_mix, gq_part, gq_send, gq_recv, gqx_send, gqx_recv,
    g_v, g_recv, o_send, t1, p_v, s_send, s_recv, rs_send, rs_recv, dw_own, dw_near, dwx_send, dwx_recv, dw_out, signs, table,
    send_sems, recv_sems, local_sems,
):
    d = lax.axis_index("dp")
    n = lax.axis_index("tensor")
    X, Y, C = d // 8, (d // 2) % 4, d % 2
    h, z = n // 4, n % 4

    def at(x, y, c):
        return ((x * 4 + y) * 2 + c, n)

    def member(delta):
        return (n + delta) % 8

    sibling = at(X, Y, 1 - C)
    x_side = at(1 - X, Y, C)
    x_across = (((1 - X) * 4 + Y) * 2 + C, (n + 4) % 8)
    y_up, y_down = at(X, (Y + 1) % 4, C), at(X, (Y + 3) % 4, C)
    z_up, z_down = (d, h * 4 + (z + 1) % 4), (d, h * 4 + (z + 3) % 4)
    own = pl.ds(pl.multiple_of(X * NH, 128), NH)
    oth = pl.ds(pl.multiple_of((1 - X) * NH, 128), NH)
    cols = (own, oth)

    def columns(hf, c):
        base = (X if hf == 0 else 1 - X) * NH
        return pl.ds(pl.multiple_of(base + CHUNKS[c][0], 128), CHUNKS[c][1])

    started = []
    count = [0, 0]

    def remote(src, dst, device):
        i = count[0]
        count[0] += 1
        copy = pltpu.make_async_remote_copy(
            src_ref=src, dst_ref=dst, send_sem=send_sems.at[i], recv_sem=recv_sems.at[i], device_id=device, device_id_type=MESH
        )
        copy.start()
        started.append(copy)
        return copy

    def local(src, dst):
        i = count[1]
        count[1] += 1
        copy = pltpu.make_async_copy(src, dst, local_sems.at[i])
        copy.start()
        return copy

    def slice_rows(zz):
        return pl.ds(pl.multiple_of(zz * QT, QT), QT)

    barrier = pltpu.get_barrier_semaphore()
    partners = [sibling, x_side, x_across, y_up, y_down] + [(d, member(delta)) for delta in range(1, 8)]
    for partner in partners:
        pl.semaphore_signal(barrier, inc=1, device_id=partner, device_id_type=MESH)

    def k_columns(xo, ry, c):
        x = X if xo == 0 else 1 - X
        return pl.ds(pl.multiple_of(((x * 4 + (Y + ry) % 4) * 2 + c) * KB, KB), KB)

    blocks = [(xo, ry) for xo in (0, 1) for ry in (0, 1, 3, 2)]
    go_own = [local(go.at[:, k_columns(xo, ry, C)], go_buf.at[pl.ds(rslot(0, 0), TB), pl.ds(kslot(xo, ry), KB)]) for xo, ry in blocks]
    w_own = local(w.at[:, own], w_buf.at[pl.ds(kslot(0, 0), KB)])
    qa_own = local(qa.at[:, own], qa_buf.at[pl.ds(rslot(0, 0), TB)])
    qa_oth_in = local(qa.at[:, oth], qa_oth)
    a_own = [local(act.at[slice_rows(z), cols[hf]], a_recv.at[z, hf]) for hf in (0, 1)]
    mask_in = [local(mask.at[:, cols[hf]], mask_v.at[hf]) for hf in (0, 1)]
    wmask_in = [local(wmask.at[:, cols[hf]], wmask_v.at[hf]) for hf in (0, 1)]
    pl.semaphore_wait(barrier, len(partners))

    def inner(c):
        return pl.ds(*CHUNKS[c])

    def w_cross(c):
        return remote(w.at[:, columns(1, c)], w_buf.at[pl.ds(kslot(1, 0), KB), inner(c)], x_side)

    def w_first(c, ry, device):
        return remote(w.at[:, columns(0, c)], w_buf.at[pl.ds(kslot(0, ry), KB), inner(c)], device)

    def w_pass(c, xo, come, go_to, device):
        here = w_buf.at[pl.ds(kslot(xo, come), KB), inner(c)]
        return remote(here, w_buf.at[pl.ds(kslot(xo, go_to), KB), inner(c)], device)

    w_x, w_up0, w_down0, w_up1, w_down1, w_far0, w_far1 = ([None] * 3 for _ in range(7))
    def w_own_pair(c):
        w_up0[c] = w_first(c, 3, y_up)
        w_down0[c] = w_first(c, 1, y_down)

    def w_pass_pair(c):
        w_x[c].wait_recv()
        w_up1[c] = w_pass(c, 1, 0, 3, y_up)
        w_down1[c] = w_pass(c, 1, 0, 1, y_down)

    def w_up_on(c):
        w_up0[c].wait_recv()
        w_far0[c] = w_pass(c, 0, 3, 2, y_up)

    def w_down_on(c):
        w_down1[c].wait_recv()
        w_far1[c] = w_pass(c, 1, 1, 2, y_down)

    def w_complete(c):
        for copy in (w_down0[c], w_up1[c], w_far0[c], w_far1[c]):
            copy.wait_recv()

    w_x[0] = w_cross(0)
    w_own_pair(0)
    go_sib = [
        remote(go.at[:, k_columns(xo, ry, 1 - C)], go_buf.at[pl.ds(rslot(0, 1), TB), pl.ds(kslot(xo, ry), KB)], sibling)
        for xo, ry in blocks
    ]
    a_in = [
        remote(act.at[slice_rows((z + delta) % 4), cols[hf]], a_recv.at[z, hf], (d, h * 4 + (z + delta) % 4))
        for delta in (1, 2, 3)
        for hf in (0, 1)
    ]
    qa_sib = remote(qa.at[:, own], qa_buf.at[pl.ds(rslot(0, 1), TB)], sibling)

    bits = lax.broadcasted_iota(jnp.int32, (GROUP, GROUP), 0) & lax.broadcasted_iota(jnp.int32, (GROUP, GROUP), 1)
    bits = bits ^ (bits >> 4)
    bits = bits ^ (bits >> 2)
    bits = bits ^ (bits >> 1)
    signs[...] = (1 - 2 * (bits & 1)).astype(F32).astype(BF16)
    for hf in (0, 1):
        first = (X if hf == 0 else 1 - X) * GH
        group = lax.broadcasted_iota(jnp.int32, (NH, GROUP), 0) // GROUP + first
        table[hf] = (group == lax.broadcasted_iota(jnp.int32, (NH, GROUP), 1)).astype(F32).astype(BF16)

    def quarter(xo, co, zz):
        return pl.ds(pl.multiple_of(rslot(xo, co) + (zz % 4) * QT, QT), QT)

    def go_cross(co):
        return [
            remote(
                go_buf.at[quarter(0, co, z), pl.ds(xo * 4 * KB, 4 * KB)],
                go_buf.at[quarter(1, co, z), pl.ds((1 - xo) * 4 * KB, 4 * KB)],
                x_across,
            )
            for xo in (0, 1)
        ]

    def go_along(co):
        for copy in go_x[co]:
            copy.wait_recv()
        here = go_buf.at[quarter(1, co, z)]
        return remote(here, here, z_up), remote(here, here, z_down)

    for copy in go_own:
        copy.wait()
    go_x = [go_cross(0), None]
    w_x[1] = w_cross(1)
    w_own_pair(1)
    for copy in go_sib:
        copy.wait_recv()
    go_x[1] = go_cross(1)
    w_pass_pair(0)
    w_x[2] = w_cross(2)
    w_up_on(0)
    go_up, go_down = [None, None], [None, None]
    go_up[0], go_down[0] = go_along(0)
    w_pass_pair(1)
    qa_x = remote(qa.at[:, oth], qa_buf.at[pl.ds(rslot(1, 0), TB)], x_side)
    w_down_on(0)
    w_up_on(1)
    w_own_pair(2)
    go_up[1], go_down[1] = go_along(1)

    for copy in a_own:
        copy.wait()
    for copy in a_in:
        copy.wait_recv()
    for hf in (0, 1):
        mixed = hadamard4(*[a_recv[zz, hf].astype(F32) for zz in range(4)])
        for zz in range(4):
            a_mix[zz, hf] = mixed[zz]

    w_pass_pair(2)

    def quant_rows(xo, co, c):
        first, width = CHUNKS[c]
        return jnp.dot(
            go_buf[rslot(xo, co) : rslot(xo, co) + TB], w_buf[:, first : first + width], preferred_element_type=F32
        )

    gq_sib = {}

    def quant_start(xo, c):
        part = slice(CHUNKS[c][0], sum(CHUNKS[c]))
        gq_send[xo, :, part] = quant_rows(xo, 1, c).astype(BF16)
        gq_sib[xo, c] = remote(gq_send.at[xo, :, inner(c)], gq_recv.at[xo, :, inner(c)], sibling)
        gq_part[xo, :, part] = quant_rows(xo, 0, c)

    def quant_end(xo, c):
        part = slice(CHUNKS[c][0], sum(CHUNKS[c]))
        gq_sib[xo, c].wait_recv()
        return (gq_part[xo, :, part] + gq_recv[xo, :, part].astype(F32)).astype(BF16)

    gq_x = [None] * 3

    def quant_cross(c):
        part = slice(CHUNKS[c][0], sum(CHUNKS[c]))
        gqx_send[:, part] = quant_end(1, c)
        gq_x[c] = remote(gqx_send.at[:, inner(c)], gqx_recv.at[:, inner(c)], x_side)

    g_in = {}

    def rotate(hf, c, quant):
        first, width = CHUNKS[c]
        part = slice(first, first + width)
        wide = quant.astype(F32)
        rot = (wide * mask_v[hf, :, part].astype(F32)).astype(BF16)
        for g in range(width // GROUP):
            g_v[hf, :, first + g * GROUP : first + (g + 1) * GROUP] = jnp.dot(
                rot[:, g * GROUP : (g + 1) * GROUP], signs[...], preferred_element_type=F32
            ).astype(BF16)
        copies = []
        for delta in range(1, 8):
            to = member(delta)
            copies.append(remote(g_v.at[hf, slice_rows(to % 4), inner(c)], g_recv.at[n, hf, :, inner(c)], (d, to)))
        g_in[hf, c] = copies, local(g_v.at[hf, slice_rows(z), inner(c)], g_recv.at[n, hf, :, inner(c)])
        quantized = qa_buf[0:TB, part] if hf == 0 else qa_oth[:, part]
        sums = group_sums(wide * quantized.astype(F32), table[hf, part])
        if hf == 0 and c == 0:
            t1[...] = sums
        else:
            t1[...] += sums

    def weight_block(xo, ry):
        return lax.dot_general(
            go_buf[:, kslot(xo, ry) : kslot(xo, ry) + KB], qa_buf[...], (((0,), (0,)), ((), ())), preferred_element_type=F32
        )

    rs_far, rs_alone, rs_added = {}, {}, {}

    def reduce_far(xo):
        rs_send[xo, 0] = weight_block(xo, 2).astype(BF16)
        rs_far[xo] = [
            remote(rs_send.at[xo, 0, pl.ds(i * HB, HB)], rs_recv.at[xo, 0, pl.ds(i * HB, HB)], (y_up, y_down)[i]) for i in (0, 1)
        ]

    def reduce_near(xo):
        rs_alone[xo] = []
        for i, ry in ((0, 1), (1, 3)):
            value = weight_block(xo, ry)
            dw_near[xo, i] = value[i * HB : (i + 1) * HB]
            rs_send[xo, 1 + i, (1 - i) * HB : (2 - i) * HB] = value[(1 - i) * HB : (2 - i) * HB].astype(BF16)
            part = pl.ds((1 - i) * HB, HB)
            rs_alone[xo].append(remote(rs_send.at[xo, 1 + i, part], rs_recv.at[xo, 1 + i, part], (y_up, y_down)[i]))

    def reduce_pass(xo):
        rs_added[xo] = []
        for i in (0, 1):
            rs_far[xo][i].wait_recv()
            rows = slice(i * HB, (i + 1) * HB)
            rs_send[xo, 1 + i, rows] = (dw_near[xo, i] + rs_recv[xo, 0, rows].astype(F32)).astype(BF16)
            part = pl.ds(i * HB, HB)
            rs_added[xo].append(remote(rs_send.at[xo, 1 + i, part], rs_recv.at[xo, 1 + i, part], (y_up, y_down)[i]))

    def reduce_end(xo):
        for copy in rs_alone[xo] + rs_added[xo]:
            copy.wait_recv()
        return dw_own[xo] + rs_recv[xo, 1].astype(F32) + rs_recv[xo, 2].astype(F32)

    w_own.wait()
    w_complete(0)
    quant_start(0, 0)
    w_down_on(1)
    go_up[0].wait_recv()
    passed = go_buf.at[quarter(1, 0, z + 3)]
    go_far0 = remote(passed, passed, z_up)
    for copy in mask_in:
        copy.wait()
    qa_own.wait()
    qa_oth_in.wait()
    rotate(0, 0, quant_end(0, 0))
    w_up_on(2)
    go_down[1].wait_recv()
    passed = go_buf.at[quarter(1, 1, z + 1)]
    go_far1 = remote(passed, passed, z_down)
    qa_x.wait_recv()
    qa_far = remote(qa_buf.at[pl.ds(rslot(1, 0), TB)], qa_buf.at[pl.ds(rslot(1, 1), TB)], sibling)
    w_complete(1)
    quant_start(0, 1)
    w_down_on(2)
    rotate(0, 1, quant_end(0, 1))
    for copy in (go_down[0], go_up[1], go_far0, go_far1):
        copy.wait_recv()
    quant_start(1, 0)
    qa_sib.wait_recv()
    qa_far.wait_recv()
    reduce_far(1)
    quant_cross(0)
    quant_start(1, 1)
    reduce_near(1)
    quant_cross(1)
    w_complete(2)
    quant_start(0, 2)
    quant_start(1, 2)
    rotate(0, 2, quant_end(0, 2))
    quant_cross(2)
    reduce_far(0)
    reduce_pass(1)
    gq_x[0].wait_recv()
    rotate(1, 0, gqx_recv[:, CHUNKS[0][0] : sum(CHUNKS[0])])
    reduce_near(0)
    dw_own[1] = weight_block(1, 0)
    gq_x[1].wait_recv()
    rotate(1, 1, gqx_recv[:, CHUNKS[1][0] : sum(CHUNKS[1])])
    dw_own[0] = weight_block(0, 0)

    sign = (1 - 2 * h).astype(F32)

    o_in = []

    def mix(hf, c):
        first, width = CHUNKS[c]
        part = slice(first, first + width)
        copies, kept = g_in[hf, c]
        for copy in copies:
            copy.wait_recv()
        kept.wait()
        sums = []
        for zz in range(4):
            sums.append(g_recv[zz, hf, :, part].astype(F32) + sign * g_recv[4 + zz, hf, :, part].astype(F32))
        mixed = hadamard4(*sums)
        for zz in range(4):
            o_send[zz, hf, :, part] = (mixed[zz] * (1.0 / 32.0)).astype(BF16)
        copies = []
        for delta in (1, 2, 3):
            to = (z + delta) % 4
            copies.append(remote(o_send.at[to, hf, :, inner(c)], out_act.at[slice_rows(z), columns(hf, c)], (d, h * 4 + to)))
        o_in.append((copies, local(o_send.at[z, hf, :, inner(c)], out_act.at[slice_rows(z), columns(hf, c)])))
        for m in range(8):
            value = g_recv[m, hf, :, part].astype(F32) * a_mix[m % 4, hf, :, part]
            top = value.astype(BF16)
            rows = slice(m * QT, (m + 1) * QT)
            p_v[0, rows, part] = top
            p_v[1, rows, part] = (value - top.astype(F32)).astype(BF16)
        sums = jnp.dot(p_v[0, :, part], table[hf, part], preferred_element_type=F32)
        sums += jnp.dot(p_v[1, :, part], table[hf, part], preferred_element_type=F32)
        if hf == 0 and c == 0:
            s_send[...] = sums
        else:
            s_send[...] += sums

    mix(0, 0)
    reduce_pass(0)
    gq_x[2].wait_recv()
    rotate(1, 2, gqx_recv[:, CHUNKS[2][0] : sum(CHUNKS[2])])
    mix(0, 1)
    dwx_send[...] = reduce_end(1).astype(BF16)
    dw_x = remote(dwx_send, dwx_recv, x_side)
    mix(0, 2)
    mix(1, 0)
    mix(1, 1)
    mix(1, 2)
    s_send[4 * QT :] *= sign
    s_in = [
        remote(s_send.at[pl.ds(pl.multiple_of(member(delta) * QT, QT), QT)], s_recv.at[n], (d, member(delta))) for delta in range(1, 8)
    ]
    s_kept = local(s_send.at[pl.ds(pl.multiple_of(n * QT, QT), QT)], s_recv.at[n])

    for copy in wmask_in:
        copy.wait()
    dw_out[0] = (reduce_end(0) * wmask_v[0].astype(F32)).astype(BF16)
    dw_done = [local(dw_out.at[0], out_weight.at[:, own]), None]

    dw_x.wait_recv()
    dw_out[1] = (dwx_recv[...].astype(F32) * wmask_v[1].astype(F32)).astype(BF16)
    dw_done[1] = local(dw_out.at[1], out_weight.at[:, oth])

    for copy in s_in:
        copy.wait_recv()
    s_kept.wait()
    for zz in range(4):
        rows = slice(zz * QT, (zz + 1) * QT)
        t1[rows] -= (s_recv[zz] + s_recv[4 + zz]) * (1.0 / 32.0)
    out_scale[...] = t1[...].T[: 2 * GH] / (scale[...] * (7.0 * GROUP) ** 0.5)

    for copies, kept in o_in:
        for copy in copies:
            copy.wait_recv()
        kept.wait()
    for copy in dw_done:
        copy.wait()
    for copy in started:
        copy.wait_send()


def hand_over(act, weight, out_act, out_weight, held, sems):
    parts = []
    for k, (src, dst) in enumerate(((act, out_act), (weight, out_weight))):
        for i in range(PARTS):
            rows = pl.ds(i * (TB // PARTS), TB // PARTS)
            come = pltpu.make_async_copy(src.at[rows], held.at[k, rows], sems.at[0, k, i])
            leave = pltpu.make_async_copy(held.at[k, rows], dst.at[rows], sems.at[1, k, i])
            come.start()
            parts.append((come, leave))
    for come, leave in parts:
        come.wait()
        leave.start()
    for come, leave in parts:
        leave.wait()


def shards(activations, quant_act, act_scale, act_mask, quant_weight, weight_mask, grad_out):
    anywhere = pl.BlockSpec(memory_space=pl.ANY)
    vmem = pl.BlockSpec(memory_space=pltpu.VMEM)
    half = (TB, NH)
    grad_act, grad_scale, grad_weight = pl.pallas_call(
        kernel,
        out_shape=(
            jax.ShapeDtypeStruct((TB, 2 * NH), BF16),
            jax.ShapeDtypeStruct((2 * GH, TB), F32),
            jax.ShapeDtypeStruct((TB, 2 * NH), BF16),
        ),
        in_specs=[anywhere, anywhere, vmem, anywhere, anywhere, anywhere, anywhere],
        out_specs=(anywhere, vmem, anywhere),
        scratch_shapes=[
            pltpu.VMEM((4 * TB, 8 * KB), BF16),
            pltpu.VMEM((8 * KB, NH), BF16),
            pltpu.VMEM((4 * TB, NH), BF16),
            pltpu.VMEM(half, BF16),
            pltpu.VMEM((2,) + half, jnp.int32),
            pltpu.VMEM((2,) + half, jnp.int32),
            pltpu.VMEM((4, 2, QT, NH), BF16),
            pltpu.VMEM((4, 2, QT, NH), F32),
            pltpu.VMEM((2,) + half, F32),
            pltpu.VMEM((2,) + half, BF16),
            pltpu.VMEM((2,) + half, BF16),
            pltpu.VMEM(half, BF16),
            pltpu.VMEM(half, BF16),
            pltpu.VMEM((2,) + half, BF16),
            pltpu.VMEM((8, 2, QT, NH), BF16),
            pltpu.VMEM((4, 2, QT, NH), BF16),
            pltpu.VMEM((TB, GROUP), F32),
            pltpu.VMEM((2, 8 * QT, NH), BF16),
            pltpu.VMEM((8 * QT, GROUP), F32),
            pltpu.VMEM((8, QT, GROUP), F32),
            pltpu.VMEM((2, 3) + half, BF16),
            pltpu.VMEM((2, 3) + half, BF16),
            pltpu.VMEM((2,) + half, F32),
            pltpu.VMEM((2, 2, HB, NH), F32),
            pltpu.VMEM(half, BF16),
            pltpu.VMEM(half, BF16),
            pltpu.VMEM((2,) + half, BF16),
            pltpu.VMEM((GROUP, GROUP), BF16),
            pltpu.VMEM((2, NH, GROUP), BF16),
            pltpu.SemaphoreType.DMA((176,)),
            pltpu.SemaphoreType.DMA((176,)),
            pltpu.SemaphoreType.DMA((32,)),
        ],
        compiler_params=pltpu.CompilerParams(collective_id=0, has_side_effects=True, vmem_limit_bytes=56 * 2**20),
        cost_estimate=pl.CostEstimate(flops=7516192768, bytes_accessed=16 * 2**20, transcendentals=0),
    )(activations, quant_act, act_scale.T, act_mask, quant_weight, weight_mask, grad_out)
    grad_act, grad_weight = pl.pallas_call(
        hand_over,
        out_shape=(jax.ShapeDtypeStruct((TB, 2 * NH), BF16),) * 2,
        in_specs=[anywhere] * 2,
        out_specs=(anywhere,) * 2,
        scratch_shapes=[
            pltpu.VMEM((2, TB, 2 * NH), BF16),
            pltpu.SemaphoreType.DMA((2, 2, PARTS)),
        ],
        cost_estimate=pl.CostEstimate(flops=0, bytes_accessed=4 * TB * 2 * NH * 2, transcendentals=0),
    )(grad_act, grad_weight)
    return grad_act, grad_scale.T, grad_weight


def solution(mesh):
    return jax.shard_map(
        shards,
        mesh=mesh,
        in_specs=(
            P("dp", "tensor"),
            P("dp", "tensor"),
            P("dp", "tensor"),
            P("dp", "tensor"),
            P("dp", "tensor"),
            P("dp", "tensor"),
            P("dp", None),
        ),
        out_specs=(P("dp", "tensor"), P("dp", "tensor"), P("dp", "tensor")),
        check_vma=False,
    )
```

```python
import functools

import jax
import jax.numpy as jnp
from jax import lax
from jax.experimental import pallas as pl
from jax.experimental.pallas import tpu as pltpu
from jax.sharding import PartitionSpec as P

TB = 256
NH = 896
KB = 256
HB = 128
GROUP = 128
QT = 64
GH = NH // GROUP
CHUNKS = ((0, 256), (256, 256), (512, 384))
PARTS = 4
MESH = pl.DeviceIdType.MESH
F32 = jnp.float32
BF16 = jnp.bfloat16
KPOS = {0: 0, 1: 1, 3: 2, 2: 3}


def kslot(xo, ry):
    return (xo * 4 + KPOS[ry]) * KB


def rslot(xo, co):
    return (xo * 2 + co) * TB


def group_sums(values, table):
    high = values.astype(BF16)
    low = (values - high.astype(F32)).astype(BF16)
    return jnp.dot(high, table, preferred_element_type=F32) + jnp.dot(low, table, preferred_element_type=F32)


def hadamard4(v0, v1, v2, v3):
    a, b, c, d = v0 + v1, v0 - v1, v2 + v3, v2 - v3
    return a + c, b + d, a - c, b - d


def kernel(
    act, qa, scale, mask, w, wmask, go,
    out_act, out_scale, out_weight,
    go_buf, w_buf, qa_buf, qa_oth, mask_v, wmask_v, a_recv, a_mix, gq_part, gq_send, gq_recv, gqx_send, gqx_recv,
    g_v, g_recv, o_send, t1, p_v, s_send, s_recv, rs_send, rs_recv, dw_own, dw_near, dwx_send, dwx_recv, dw_out, signs, table,
    send_sems, recv_sems, local_sems,
):
    d = lax.axis_index("dp")
    n = lax.axis_index("tensor")
    X, Y, C = d // 8, (d // 2) % 4, d % 2
    h, z = n // 4, n % 4

    def at(x, y, c):
        return ((x * 4 + y) * 2 + c, n)

    def member(delta):
        return (n + delta) % 8

    sibling = at(X, Y, 1 - C)
    x_side = at(1 - X, Y, C)
    x_across = (((1 - X) * 4 + Y) * 2 + C, (n + 4) % 8)
    y_up, y_down = at(X, (Y + 1) % 4, C), at(X, (Y + 3) % 4, C)
    z_up, z_down = (d, h * 4 + (z + 1) % 4), (d, h * 4 + (z + 3) % 4)
    own = pl.ds(pl.multiple_of(X * NH, 128), NH)
    oth = pl.ds(pl.multiple_of((1 - X) * NH, 128), NH)
    cols = (own, oth)

    def columns(hf, c):
        base = (X if hf == 0 else 1 - X) * NH
        return pl.ds(pl.multiple_of(base + CHUNKS[c][0], 128), CHUNKS[c][1])

    started = []
    count = [0, 0]

    def remote(src, dst, device):
        i = count[0]
        count[0] += 1
        copy = pltpu.make_async_remote_copy(
            src_ref=src, dst_ref=dst, send_sem=send_sems.at[i], recv_sem=recv_sems.at[i], device_id=device, device_id_type=MESH
        )
        copy.start()
        started.append(copy)
        return copy

    def local(src, dst):
        i = count[1]
        count[1] += 1
        copy = pltpu.make_async_copy(src, dst, local_sems.at[i])
        copy.start()
        return copy

    def slice_rows(zz):
        return pl.ds(pl.multiple_of(zz * QT, QT), QT)

    barrier = pltpu.get_barrier_semaphore()
    partners = [sibling, x_side, x_across, y_up, y_down] + [(d, member(delta)) for delta in range(1, 8)]
    for partner in partners:
        pl.semaphore_signal(barrier, inc=1, device_id=partner, device_id_type=MESH)

    def k_columns(xo, ry, c):
        x = X if xo == 0 else 1 - X
        return pl.ds(pl.multiple_of(((x * 4 + (Y + ry) % 4) * 2 + c) * KB, KB), KB)

    blocks = [(xo, ry) for xo in (0, 1) for ry in (0, 1, 3, 2)]
    go_own = [local(go.at[:, k_columns(xo, ry, C)], go_buf.at[pl.ds(rslot(0, 0), TB), pl.ds(kslot(xo, ry), KB)]) for xo, ry in blocks]
    w_own = local(w.at[:, own], w_buf.at[pl.ds(kslot(0, 0), KB)])
    qa_own = local(qa.at[:, own], qa_buf.at[pl.ds(rslot(0, 0), TB)])
    qa_oth_in = local(qa.at[:, oth], qa_oth)
    a_own = [local(act.at[slice_rows(z), cols[hf]], a_recv.at[z, hf]) for hf in (0, 1)]
    mask_in = [local(mask.at[:, cols[hf]], mask_v.at[hf]) for hf in (0, 1)]
    wmask_in = [local(wmask.at[:, cols[hf]], wmask_v.at[hf]) for hf in (0, 1)]
    pl.semaphore_wait(barrier, len(partners))

    def inner(c):
        return pl.ds(*CHUNKS[c])

    def w_cross(c):
        return remote(w.at[:, columns(1, c)], w_buf.at[pl.ds(kslot(1, 0), KB), inner(c)], x_side)

    def w_first(c, ry, device):
        return remote(w.at[:, columns(0, c)], w_buf.at[pl.ds(kslot(0, ry), KB), inner(c)], device)

    def w_pass(c, xo, come, go_to, device):
        here = w_buf.at[pl.ds(kslot(xo, come), KB), inner(c)]
        return remote(here, w_buf.at[pl.ds(kslot(xo, go_to), KB), inner(c)], device)

    w_x, w_up0, w_down0, w_up1, w_down1, w_far0, w_far1 = ([None] * 3 for _ in range(7))
    def w_own_pair(c):
        w_up0[c] = w_first(c, 3, y_up)
        w_down0[c] = w_first(c, 1, y_down)

    def w_pass_pair(c):
        w_x[c].wait_recv()
        w_up1[c] = w_pass(c, 1, 0, 3, y_up)
        w_down1[c] = w_pass(c, 1, 0, 1, y_down)

    def w_up_on(c):
        w_up0[c].wait_recv()
        w_far0[c] = w_pass(c, 0, 3, 2, y_up)

    def w_down_on(c):
        w_down1[c].wait_recv()
        w_far1[c] = w_pass(c, 1, 1, 2, y_down)

    def w_complete(c):
        for copy in (w_down0[c], w_up1[c], w_far0[c], w_far1[c]):
            copy.wait_recv()

    w_x[0] = w_cross(0)
    w_own_pair(0)
    go_sib = [
        remote(go.at[:, k_columns(xo, ry, 1 - C)], go_buf.at[pl.ds(rslot(0, 1), TB), pl.ds(kslot(xo, ry), KB)], sibling)
        for xo, ry in blocks
    ]
    a_in = [
        remote(act.at[slice_rows((z + delta) % 4), cols[hf]], a_recv.at[z, hf], (d, h * 4 + (z + delta) % 4))
        for delta in (1, 2, 3)
        for hf in (0, 1)
    ]
    qa_sib = remote(qa.at[:, own], qa_buf.at[pl.ds(rslot(0, 1), TB)], sibling)

    bits = lax.broadcasted_iota(jnp.int32, (GROUP, GROUP), 0) & lax.broadcasted_iota(jnp.int32, (GROUP, GROUP), 1)
    bits = bits ^ (bits >> 4)
    bits = bits ^ (bits >> 2)
    bits = bits ^ (bits >> 1)
    signs[...] = (1 - 2 * (bits & 1)).astype(F32).astype(BF16)
    for hf in (0, 1):
        first = (X if hf == 0 else 1 - X) * GH
        group = lax.broadcasted_iota(jnp.int32, (NH, GROUP), 0) // GROUP + first
        table[hf] = (group == lax.broadcasted_iota(jnp.int32, (NH, GROUP), 1)).astype(F32).astype(BF16)

    def quarter(xo, co, zz):
        return pl.ds(pl.multiple_of(rslot(xo, co) + (zz % 4) * QT, QT), QT)

    def go_cross(co):
        return [
            remote(
                go_buf.at[quarter(0, co, z), pl.ds(xo * 4 * KB, 4 * KB)],
                go_buf.at[quarter(1, co, z), pl.ds((1 - xo) * 4 * KB, 4 * KB)],
                x_across,
            )
            for xo in (0, 1)
        ]

    def go_along(co):
        for copy in go_x[co]:
            copy.wait_recv()
        here = go_buf.at[quarter(1, co, z)]
        return remote(here, here, z_up), remote(here, here, z_down)

    for copy in go_own:
        copy.wait()
    go_x = [go_cross(0), None]
    w_x[1] = w_cross(1)
    w_own_pair(1)
    for copy in go_sib:
        copy.wait_recv()
    go_x[1] = go_cross(1)
    w_pass_pair(0)
    w_x[2] = w_cross(2)
    w_up_on(0)
    go_up, go_down = [None, None], [None, None]
    go_up[0], go_down[0] = go_along(0)
    w_pass_pair(1)
    qa_x = remote(qa.at[:, oth], qa_buf.at[pl.ds(rslot(1, 0), TB)], x_side)
    w_down_on(0)
    w_up_on(1)
    w_own_pair(2)
    go_up[1], go_down[1] = go_along(1)

    for copy in a_own:
        copy.wait()
    for copy in a_in:
        copy.wait_recv()
    for hf in (0, 1):
        mixed = hadamard4(*[a_recv[zz, hf].astype(F32) for zz in range(4)])
        for zz in range(4):
            a_mix[zz, hf] = mixed[zz]

    w_pass_pair(2)

    def quant_rows(xo, co, c):
        first, width = CHUNKS[c]
        return jnp.dot(
            go_buf[rslot(xo, co) : rslot(xo, co) + TB], w_buf[:, first : first + width], preferred_element_type=F32
        )

    gq_sib = {}

    def quant_start(xo, c):
        part = slice(CHUNKS[c][0], sum(CHUNKS[c]))
        gq_send[xo, :, part] = quant_rows(xo, 1, c).astype(BF16)
        gq_sib[xo, c] = remote(gq_send.at[xo, :, inner(c)], gq_recv.at[xo, :, inner(c)], sibling)
        gq_part[xo, :, part] = quant_rows(xo, 0, c)

    def quant_end(xo, c):
        part = slice(CHUNKS[c][0], sum(CHUNKS[c]))
        gq_sib[xo, c].wait_recv()
        return (gq_part[xo, :, part] + gq_recv[xo, :, part].astype(F32)).astype(BF16)

    gq_x = [None] * 3

    def quant_cross(c):
        part = slice(CHUNKS[c][0], sum(CHUNKS[c]))
        gqx_send[:, part] = quant_end(1, c)
        gq_x[c] = remote(gqx_send.at[:, inner(c)], gqx_recv.at[:, inner(c)], x_side)

    g_in = {}

    def rotate(hf, c, quant):
        first, width = CHUNKS[c]
        part = slice(first, first + width)
        wide = quant.astype(F32)
        rot = (wide * mask_v[hf, :, part].astype(F32)).astype(BF16)
        for g in range(width // GROUP):
            g_v[hf, :, first + g * GROUP : first + (g + 1) * GROUP] = jnp.dot(
                rot[:, g * GROUP : (g + 1) * GROUP], signs[...], preferred_element_type=F32
            ).astype(BF16)
        copies = []
        for delta in range(1, 8):
            to = member(delta)
            copies.append(remote(g_v.at[hf, slice_rows(to % 4), inner(c)], g_recv.at[n, hf, :, inner(c)], (d, to)))
        g_in[hf, c] = copies, local(g_v.at[hf, slice_rows(z), inner(c)], g_recv.at[n, hf, :, inner(c)])
        quantized = qa_buf[0:TB, part] if hf == 0 else qa_oth[:, part]
        sums = group_sums(wide * quantized.astype(F32), table[hf, part])
        if hf == 0 and c == 0:
            t1[...] = sums
        else:
            t1[...] += sums

    def weight_block(xo, ry):
        return lax.dot_general(
            go_buf[:, kslot(xo, ry) : kslot(xo, ry) + KB], qa_buf[...], (((0,), (0,)), ((), ())), preferred_element_type=F32
        )

    rs_far, rs_alone, rs_added = {}, {}, {}

    def reduce_far(xo):
        rs_send[xo, 0] = weight_block(xo, 2).astype(BF16)
        rs_far[xo] = [
            remote(rs_send.at[xo, 0, pl.ds(i * HB, HB)], rs_recv.at[xo, 0, pl.ds(i * HB, HB)], (y_up, y_down)[i]) for i in (0, 1)
        ]

    def reduce_near(xo):
        rs_alone[xo] = []
        for i, ry in ((0, 1), (1, 3)):
            value = weight_block(xo, ry)
            dw_near[xo, i] = value[i * HB : (i + 1) * HB]
            rs_send[xo, 1 + i, (1 - i) * HB : (2 - i) * HB] = value[(1 - i) * HB : (2 - i) * HB].astype(BF16)
            part = pl.ds((1 - i) * HB, HB)
            rs_alone[xo].append(remote(rs_send.at[xo, 1 + i, part], rs_recv.at[xo, 1 + i, part], (y_up, y_down)[i]))

    def reduce_pass(xo):
        rs_added[xo] = []
        for i in (0, 1):
            rs_far[xo][i].wait_recv()
            rows = slice(i * HB, (i + 1) * HB)
            rs_send[xo, 1 + i, rows] = (dw_near[xo, i] + rs_recv[xo, 0, rows].astype(F32)).astype(BF16)
            part = pl.ds(i * HB, HB)
            rs_added[xo].append(remote(rs_send.at[xo, 1 + i, part], rs_recv.at[xo, 1 + i, part], (y_up, y_down)[i]))

    def reduce_end(xo):
        for copy in rs_alone[xo] + rs_added[xo]:
            copy.wait_recv()
        return dw_own[xo] + rs_recv[xo, 1].astype(F32) + rs_recv[xo, 2].astype(F32)

    w_own.wait()
    w_complete(0)
    quant_start(0, 0)
    w_down_on(1)
    go_up[0].wait_recv()
    passed = go_buf.at[quarter(1, 0, z + 3)]
    go_far0 = remote(passed, passed, z_up)
    for copy in mask_in:
        copy.wait()
    qa_own.wait()
    qa_oth_in.wait()
    rotate(0, 0, quant_end(0, 0))
    w_up_on(2)
    go_down[1].wait_recv()
    passed = go_buf.at[quarter(1, 1, z + 1)]
    go_far1 = remote(passed, passed, z_down)
    qa_x.wait_recv()
    qa_far = remote(qa_buf.at[pl.ds(rslot(1, 0), TB)], qa_buf.at[pl.ds(rslot(1, 1), TB)], sibling)
    w_complete(1)
    quant_start(0, 1)
    w_down_on(2)
    rotate(0, 1, quant_end(0, 1))
    for copy in (go_down[0], go_up[1], go_far0, go_far1):
        copy.wait_recv()
    quant_start(1, 0)
    qa_sib.wait_recv()
    qa_far.wait_recv()
    reduce_far(1)
    quant_cross(0)
    quant_start(1, 1)
    reduce_near(1)
    quant_cross(1)
    w_complete(2)
    quant_start(0, 2)
    quant_start(1, 2)
    rotate(0, 2, quant_end(0, 2))
    quant_cross(2)
    reduce_far(0)
    gq_x[0].wait_recv()
    rotate(1, 0, gqx_recv[:, CHUNKS[0][0] : sum(CHUNKS[0])])
    reduce_pass(1)
    reduce_near(0)
    dw_own[1] = weight_block(1, 0)
    gq_x[1].wait_recv()
    rotate(1, 1, gqx_recv[:, CHUNKS[1][0] : sum(CHUNKS[1])])
    dw_own[0] = weight_block(0, 0)

    sign = (1 - 2 * h).astype(F32)

    o_in = []

    def mix(hf, c):
        first, width = CHUNKS[c]
        part = slice(first, first + width)
        copies, kept = g_in[hf, c]
        for copy in copies:
            copy.wait_recv()
        kept.wait()
        sums = []
        for zz in range(4):
            sums.append(g_recv[zz, hf, :, part].astype(F32) + sign * g_recv[4 + zz, hf, :, part].astype(F32))
        mixed = hadamard4(*sums)
        for zz in range(4):
            o_send[zz, hf, :, part] = (mixed[zz] * (1.0 / 32.0)).astype(BF16)
        copies = []
        for delta in (1, 2, 3):
            to = (z + delta) % 4
            copies.append(remote(o_send.at[to, hf, :, inner(c)], out_act.at[slice_rows(z), columns(hf, c)], (d, h * 4 + to)))
        o_in.append((copies, local(o_send.at[z, hf, :, inner(c)], out_act.at[slice_rows(z), columns(hf, c)])))
        for m in range(8):
            value = g_recv[m, hf, :, part].astype(F32) * a_mix[m % 4, hf, :, part]
            top = value.astype(BF16)
            rows = slice(m * QT, (m + 1) * QT)
            p_v[0, rows, part] = top
            p_v[1, rows, part] = (value - top.astype(F32)).astype(BF16)
        sums = jnp.dot(p_v[0, :, part], table[hf, part], preferred_element_type=F32)
        sums += jnp.dot(p_v[1, :, part], table[hf, part], preferred_element_type=F32)
        if hf == 0 and c == 0:
            s_send[...] = sums
        else:
            s_send[...] += sums

    mix(0, 0)
    reduce_pass(0)
    gq_x[2].wait_recv()
    rotate(1, 2, gqx_recv[:, CHUNKS[2][0] : sum(CHUNKS[2])])
    mix(0, 1)
    dwx_send[...] = reduce_end(1).astype(BF16)
    dw_x = remote(dwx_send, dwx_recv, x_side)
    mix(0, 2)
    mix(1, 0)
    mix(1, 1)
    mix(1, 2)
    s_send[4 * QT :] *= sign
    s_in = [
        remote(s_send.at[pl.ds(pl.multiple_of(member(delta) * QT, QT), QT)], s_recv.at[n], (d, member(delta))) for delta in range(1, 8)
    ]
    s_kept = local(s_send.at[pl.ds(pl.multiple_of(n * QT, QT), QT)], s_recv.at[n])

    for copy in wmask_in:
        copy.wait()
    dw_out[0] = (reduce_end(0) * wmask_v[0].astype(F32)).astype(BF16)
    dw_done = [local(dw_out.at[0], out_weight.at[:, own]), None]

    dw_x.wait_recv()
    dw_out[1] = (dwx_recv[...].astype(F32) * wmask_v[1].astype(F32)).astype(BF16)
    dw_done[1] = local(dw_out.at[1], out_weight.at[:, oth])

    for copy in s_in:
        copy.wait_recv()
    s_kept.wait()
    for zz in range(4):
        rows = slice(zz * QT, (zz + 1) * QT)
        t1[rows] -= (s_recv[zz] + s_recv[4 + zz]) * (1.0 / 32.0)
    out_scale[...] = t1[...].T[: 2 * GH] / (scale[...] * (7.0 * GROUP) ** 0.5)

    for copies, kept in o_in:
        for copy in copies:
            copy.wait_recv()
        kept.wait()
    for copy in dw_done:
        copy.wait()
    for copy in started:
        copy.wait_send()


def hand_over(act, weight, out_act, out_weight, held, sems):
    parts = []
    for k, (src, dst) in enumerate(((act, out_act), (weight, out_weight))):
        for i in range(PARTS):
            rows = pl.ds(i * (TB // PARTS), TB // PARTS)
            come = pltpu.make_async_copy(src.at[rows], held.at[k, rows], sems.at[0, k, i])
            leave = pltpu.make_async_copy(held.at[k, rows], dst.at[rows], sems.at[1, k, i])
            come.start()
            parts.append((come, leave))
    for come, leave in parts:
        come.wait()
        leave.start()
    for come, leave in parts:
        leave.wait()


def shards(activations, quant_act, act_scale, act_mask, quant_weight, weight_mask, grad_out):
    anywhere = pl.BlockSpec(memory_space=pl.ANY)
    vmem = pl.BlockSpec(memory_space=pltpu.VMEM)
    half = (TB, NH)
    grad_act, grad_scale, grad_weight = pl.pallas_call(
        kernel,
        out_shape=(
            jax.ShapeDtypeStruct((TB, 2 * NH), BF16),
            jax.ShapeDtypeStruct((2 * GH, TB), F32),
            jax.ShapeDtypeStruct((TB, 2 * NH), BF16),
        ),
        in_specs=[anywhere, anywhere, vmem, anywhere, anywhere, anywhere, anywhere],
        out_specs=(anywhere, vmem, anywhere),
        scratch_shapes=[
            pltpu.VMEM((4 * TB, 8 * KB), BF16),
            pltpu.VMEM((8 * KB, NH), BF16),
            pltpu.VMEM((4 * TB, NH), BF16),
            pltpu.VMEM(half, BF16),
            pltpu.VMEM((2,) + half, jnp.int32),
            pltpu.VMEM((2,) + half, jnp.int32),
            pltpu.VMEM((4, 2, QT, NH), BF16),
            pltpu.VMEM((4, 2, QT, NH), F32),
            pltpu.VMEM((2,) + half, F32),
            pltpu.VMEM((2,) + half, BF16),
            pltpu.VMEM((2,) + half, BF16),
            pltpu.VMEM(half, BF16),
            pltpu.VMEM(half, BF16),
            pltpu.VMEM((2,) + half, BF16),
            pltpu.VMEM((8, 2, QT, NH), BF16),
            pltpu.VMEM((4, 2, QT, NH), BF16),
            pltpu.VMEM((TB, GROUP), F32),
            pltpu.VMEM((2, 8 * QT, NH), BF16),
            pltpu.VMEM((8 * QT, GROUP), F32),
            pltpu.VMEM((8, QT, GROUP), F32),
            pltpu.VMEM((2, 3) + half, BF16),
            pltpu.VMEM((2, 3) + half, BF16),
            pltpu.VMEM((2,) + half, F32),
            pltpu.VMEM((2, 2, HB, NH), F32),
            pltpu.VMEM(half, BF16),
            pltpu.VMEM(half, BF16),
            pltpu.VMEM((2,) + half, BF16),
            pltpu.VMEM((GROUP, GROUP), BF16),
            pltpu.VMEM((2, NH, GROUP), BF16),
            pltpu.SemaphoreType.DMA((176,)),
            pltpu.SemaphoreType.DMA((176,)),
            pltpu.SemaphoreType.DMA((32,)),
        ],
        compiler_params=pltpu.CompilerParams(collective_id=0, has_side_effects=True, vmem_limit_bytes=56 * 2**20),
        cost_estimate=pl.CostEstimate(flops=7516192768, bytes_accessed=16 * 2**20, transcendentals=0),
    )(activations, quant_act, act_scale.T, act_mask, quant_weight, weight_mask, grad_out)
    grad_act, grad_weight = pl.pallas_call(
        hand_over,
        out_shape=(jax.ShapeDtypeStruct((TB, 2 * NH), BF16),) * 2,
        in_specs=[anywhere] * 2,
        out_specs=(anywhere,) * 2,
        scratch_shapes=[
            pltpu.VMEM((2, TB, 2 * NH), BF16),
            pltpu.SemaphoreType.DMA((2, 2, PARTS)),
        ],
        cost_estimate=pl.CostEstimate(flops=0, bytes_accessed=4 * TB * 2 * NH * 2, transcendentals=0),
    )(grad_act, grad_weight)
    return grad_act, grad_scale.T, grad_weight


def solution(mesh):
    return jax.shard_map(
        shards,
        mesh=mesh,
        in_specs=(
            P("dp", "tensor"),
            P("dp", "tensor"),
            P("dp", "tensor"),
            P("dp", "tensor"),
            P("dp", "tensor"),
            P("dp", "tensor"),
            P("dp", None),
        ),
        out_specs=(P("dp", "tensor"), P("dp", "tensor"), P("dp", "tensor")),
        check_vma=False,
    )
```
